32 devices in a mesh: blk: 8 (over z, x), group: 4 (over y, core).
Axes of the slice: x: 2, y: 2, z: 4, core: 2. Of those that a mesh axis runs over, the one named last changes fastest.
Arguments:
- user_factors: float32 [8192, 256], P(('blk', 'group')), may hold values from -1.5 to 1.5
- user_state: float32 [8192, 256], P(('blk', 'group')), may hold values from 0.5 to 20
- item_factors: float32 [8192, 256], P(('blk', 'group')), may hold values from -1.5 to 1.5
- item_state: float32 [8192, 256], P(('blk', 'group')), may hold values from 0.5 to 20
- counts: int32 [8192, 1024], P(('blk', 'group')), may hold values from 0 to 5
Outputs:
- users_out: float32 [8192, 256], P(('blk', 'group'))
- user_state_out: float32 [8192, 256], P(('blk', 'group'))
- items_out: float32 [8192, 256], P(('blk', 'group'))
- item_state_out: float32 [8192, 256], P(('blk', 'group'))
The draws below stay inside these ranges and needn't reach their ends.
All inputs are finite; a program needn't handle non-finite values.
Results may differ from the reference program's by a relative error of at most 0.0003.
Values sent between devices are 32-bit elements; how exact they have to be, the bound alone decides.
No kernel may reach another device: no remote copies, remote signals or barrier semaphores. Data moves between devices by JAX's collectives and lax.ppermute only.
A program may use at most 64 MiB of HBM per device.

```python
import math
import jax
import jax.numpy as jnp
from jax import lax

R = 256
USERS_DEV = 256
ITEM_BLK = 256
STRATA = 4
USERS = 8192
ITEMS = 8192
N_BLK = 8
N_GROUP = 4


def plant(entries, stream_key, low, high):
    shape = entries.shape
    index_at = [jax.random.randint(jax.random.fold_in(stream_key, axis), (), 0, shape[axis]) for axis in range(len(shape))]
    entries = entries.at[tuple(index_at)].set(low)
    longest = shape.index(max(shape))
    index_at[longest] = (index_at[longest] + 1) % shape[longest]
    return entries.at[tuple(index_at)].set(high)


def block_scale(stream_key, shape, shards, least, high):
    loudness, own = 1.0, jax.random.fold_in(stream_key, 6)
    for dim, shards_of in shards:
        heights = jnp.exp(jax.random.uniform(jax.random.fold_in(own, dim), (shards_of,), jnp.float32, least / len(shards), high / len(shards)))
        loudness = loudness * jnp.repeat(heights, shape[dim] // shards_of).reshape([-1 if axis == dim else 1 for axis in range(len(shape))])
    return loudness


def centred(own_key, dims, spread, bound, split=(), kind=jnp.bfloat16):
    array = spread * jax.random.normal(own_key, dims, jnp.float32)
    if split:
        array = array * block_scale(own_key, dims, split, -0.22, 0.18)
    return jnp.clip(array, -bound, bound).astype(kind)


def setup_inputs(seed: int = 0) -> dict:
    key_list = jax.random.split(jax.random.key(seed), 6)
    user_factors = centred(key_list[0], (USERS, R), 0.25, 1.5, ((0, 32),), jnp.float32)
    user_state = jnp.clip(jnp.exp(math.log(20.0) - 3.6888795 * jax.random.uniform(key_list[1], (USERS, R), jnp.float32) ** block_scale(key_list[1], (USERS, R), ((0, 32),), -0.2, 0.2)), 0.5, 20.0)
    item_factors = centred(key_list[2], (ITEMS, R), 0.25, 1.5, ((0, 32),), jnp.float32)
    item_state = jnp.clip(jnp.exp(math.log(20.0) - 3.6888795 * jax.random.uniform(key_list[3], (ITEMS, R), jnp.float32) ** block_scale(key_list[3], (ITEMS, R), ((0, 32),), -0.2, 0.2)), 0.5, 20.0)
    counts = plant(jax.random.randint(key_list[4], (USERS, STRATA * ITEM_BLK), 0, 6), jax.random.fold_in(key_list[4], 1), 0, 5).astype(jnp.int32)
    return dict(user_factors=user_factors, user_state=user_state, item_factors=item_factors, item_state=item_state, counts=counts)


conf_scale = 0.5
ridge_weight = 0.01
step_rate = 0.1

def update_block(users, user_acc, items, item_acc, count_tile):
    highest = lax.Precision.HIGHEST
    predicted = jnp.dot(users, items.T, precision=highest)
    prefer = (count_tile > 0).astype(users.dtype)
    confidence = 1.0 + conf_scale * count_tile.astype(users.dtype)
    weighted_gap = confidence * (predicted - prefer)
    user_grad = 2.0 * jnp.dot(weighted_gap, items, precision=highest) + 2.0 * ridge_weight * users
    item_grad = 2.0 * jnp.dot(weighted_gap.T, users, precision=highest) + 2.0 * ridge_weight * items
    user_acc = user_acc + user_grad * user_grad
    item_acc = item_acc + item_grad * item_grad
    users = users - step_rate * user_grad / jnp.sqrt(user_acc)
    items = items - step_rate * item_grad / jnp.sqrt(item_acc)
    return (users, user_acc, items, item_acc)

def per_blk(packed):
    return jax.vmap(update_block)(*packed)

def reference(user_factors, user_state, item_factors, item_state, counts):
    users = user_factors.reshape(N_BLK, N_GROUP, USERS_DEV, R)
    user_acc = user_state.reshape(N_BLK, N_GROUP, USERS_DEV, R)
    items = item_factors.reshape(N_BLK, N_GROUP, ITEM_BLK, R)
    item_acc = item_state.reshape(N_BLK, N_GROUP, ITEM_BLK, R)
    count_grid = counts.reshape(N_BLK, N_GROUP, USERS_DEV, STRATA, ITEM_BLK)
    for stratum in range(STRATA):
        count_tile = count_grid[:, :, :, stratum, :]
        users, user_acc, items, item_acc = lax.map(per_blk, (users, user_acc, items, item_acc, count_tile))
        items = jnp.roll(items, 1, axis=0)
        item_acc = jnp.roll(item_acc, 1, axis=0)
    items = jnp.roll(items, 1, axis=1)
    item_acc = jnp.roll(item_acc, 1, axis=1)
    return (users.reshape(USERS, R), user_acc.reshape(USERS, R), items.reshape(ITEMS, R), item_acc.reshape(ITEMS, R))
```

```python
import jax
import jax.numpy as jnp
from jax import lax
from jax.sharding import PartitionSpec as P

conf_scale = 0.5
ridge_weight = 0.01
step_rate = 0.1

PREC = lax.Precision.HIGH


def sent(value, where):
    n_blk, n_group = lax.axis_size("blk"), lax.axis_size("group")
    pairs = []
    for b in range(n_blk):
        for g in range(n_group):
            target = where(b, g)
            if target is not None:
                pairs.append((b * n_group + g, target[0] % n_blk * n_group + target[1] % n_group))
    return lax.ppermute(value, ("blk", "group"), pairs)


def weighted_gap(users, items, count_tile):
    predicted = lax.dot_general(users, items, (((1,), (1,)), ((), ())), precision=PREC)
    prefer = (count_tile > 0).astype(jnp.float32)
    confidence = 1.0 + conf_scale * count_tile.astype(jnp.float32)
    return confidence * (predicted - prefer)


def user_gradient(gap, users, items):
    return 2.0 * jnp.dot(gap, items, precision=PREC) + 2.0 * ridge_weight * users


def item_gradient(gap, users, items):
    product = lax.dot_general(gap, users, (((0,), (0,)), ((), ())), precision=PREC)
    return 2.0 * product + 2.0 * ridge_weight * items


def adagrad(factors, sums, gradient):
    sums = sums + gradient * gradient
    return factors - step_rate * gradient / jnp.sqrt(sums), sums


def body(users, user_acc, items, item_acc, counts):
    rows = items.shape[0]
    tiles = [counts[:, s * rows : (s + 1) * rows] for s in range(4)]
    odd = lax.axis_index("blk") % 2 == 1

    def two_strata(users, user_acc, items, item_acc, first, up):
        gap = weighted_gap(users, items, tiles[first])
        grad_v = item_gradient(gap, users, items)
        grad_u = user_gradient(gap, users, items)
        items, item_acc = adagrad(items, item_acc, grad_v)
        users, user_acc = adagrad(users, user_acc, grad_u)

        visitor = sent(items, lambda b, g: (b + 1, g))
        items, item_acc, users = lax.optimization_barrier((items, item_acc, users))
        ahead = sent(jnp.where(odd, item_acc, items), lambda b, g: (b + 2, g + up))
        even_acc = sent(item_acc, lambda b, g: (b + 2, g + up) if b % 2 == 0 else None)
        passed = sent(visitor, lambda b, g: (b + 1, g + up) if b % 2 == 0 else None)
        gap = weighted_gap(users, visitor, tiles[first + 1])
        grad_v = item_gradient(gap, users, visitor)
        grad_u = user_gradient(gap, users, visitor)
        grad_v = sent(grad_v, lambda b, g: (b + 1, g + up))
        users, user_acc = adagrad(users, user_acc, grad_u)
        items = jnp.where(odd, passed, ahead)
        item_acc = jnp.where(odd, ahead, even_acc)
        items, item_acc = adagrad(items, item_acc, grad_v)
        return users, user_acc, items, item_acc

    state = two_strata(users, user_acc, items, item_acc, 0, 0)
    return two_strata(*state, 2, 1)


def solution(mesh):
    spec = P(("blk", "group"), None)
    return jax.shard_map(body, mesh=mesh, in_specs=(spec,) * 5, out_specs=(spec,) * 4, check_vma=False)
```

```python
import jax
import jax.numpy as jnp
from jax import lax
from jax.sharding import PartitionSpec as P

conf_scale = 0.5
ridge_weight = 0.01
step_rate = 0.1

PREC = lax.Precision.HIGH


def sent(value, where):
    n_blk, n_group = lax.axis_size("blk"), lax.axis_size("group")
    pairs = []
    for b in range(n_blk):
        for g in range(n_group):
            target = where(b, g)
            if target is not None:
                pairs.append((b * n_group + g, target[0] % n_blk * n_group + target[1] % n_group))
    return lax.ppermute(value, ("blk", "group"), pairs)


def weighted_gap(users, items, count_tile):
    predicted = lax.dot_general(users, items, (((1,), (1,)), ((), ())), precision=PREC)
    prefer = (count_tile > 0).astype(jnp.float32)
    confidence = 1.0 + conf_scale * count_tile.astype(jnp.float32)
    return confidence * (predicted - prefer)


def user_gradient(gap, users, items):
    return 2.0 * jnp.dot(gap, items, precision=PREC) + 2.0 * ridge_weight * users


def item_gradient(gap, users, items):
    product = lax.dot_general(gap, users, (((0,), (0,)), ((), ())), precision=PREC)
    return 2.0 * product + 2.0 * ridge_weight * items


def adagrad(factors, sums, gradient):
    sums = sums + gradient * gradient
    return factors - step_rate * gradient / jnp.sqrt(sums), sums


def body(users, user_acc, items, item_acc, counts):
    rows = items.shape[0]
    tiles = [counts[:, s * rows : (s + 1) * rows] for s in range(4)]
    odd = lax.axis_index("blk") % 2 == 1

    def two_strata(users, user_acc, items, item_acc, first, up):
        gap = weighted_gap(users, items, tiles[first])
        grad_v = item_gradient(gap, users, items)
        grad_u = user_gradient(gap, users, items)
        items, item_acc = adagrad(items, item_acc, grad_v)
        users, user_acc = adagrad(users, user_acc, grad_u)

        visitor = sent(items, lambda b, g: (b + 1, g))
        items, item_acc, users = lax.optimization_barrier((items, item_acc, users))
        ahead = sent(jnp.where(odd, item_acc, items), lambda b, g: (b + 2, g + up))
        even_acc = sent(item_acc, lambda b, g: (b + 2, g + up) if b % 2 == 0 else None)
        passed = sent(visitor, lambda b, g: (b + 1, g + up) if b % 2 == 0 else None)
        gap = weighted_gap(users, visitor, tiles[first + 1])
        grad_v = item_gradient(gap, users, visitor)
        grad_v = sent(grad_v, lambda b, g: (b + 1, g + up))
        items = jnp.where(odd, passed, ahead)
        item_acc = jnp.where(odd, ahead, even_acc)
        gap, items, item_acc = lax.optimization_barrier((gap, items, item_acc))
        users, user_acc = adagrad(users, user_acc, user_gradient(gap, users, visitor))
        users, items, item_acc, grad_v = lax.optimization_barrier((users, items, item_acc, grad_v))
        items, item_acc = adagrad(items, item_acc, grad_v)
        return users, user_acc, items, item_acc

    state = two_strata(users, user_acc, items, item_acc, 0, 0)
    return two_strata(*state, 2, 1)


def solution(mesh):
    spec = P(("blk", "group"), None)
    return jax.shard_map(body, mesh=mesh, in_specs=(spec,) * 5, out_specs=(spec,) * 4, check_vma=False)
```

```python
import jax
import jax.numpy as jnp
from jax import lax
from jax.experimental import pallas as pl
from jax.experimental.pallas import tpu as pltpu
from jax.sharding import PartitionSpec as P

conf_scale = 0.5
ridge_weight = 0.01
step_rate = 0.1

PREC = lax.Precision.HIGH


def sent(value, where):
    n_blk, n_group = lax.axis_size("blk"), lax.axis_size("group")
    pairs = []
    for b in range(n_blk):
        for g in range(n_group):
            target = where(b, g)
            if target is not None:
                pairs.append((b * n_group + g, target[0] % n_blk * n_group + target[1] % n_group))
    return lax.ppermute(value, ("blk", "group"), pairs)


def halves(value):
    high = value.astype(jnp.bfloat16)
    return high, (value - high.astype(jnp.float32)).astype(jnp.bfloat16)


def product(left, right, dims):
    def dot(a, b):
        return lax.dot_general(a, b, (dims, ((), ())), preferred_element_type=jnp.float32)

    return dot(left[0], right[1]) + dot(left[1], right[0]) + dot(left[0], right[0])


def weighted_gap(users, items, count_tile):
    predicted = lax.dot_general(users, items, (((1,), (1,)), ((), ())), precision=PREC)
    prefer = (count_tile > 0).astype(jnp.float32)
    confidence = 1.0 + conf_scale * count_tile.astype(jnp.float32)
    return confidence * (predicted - prefer)


def item_gradient(gap, users, items):
    product = lax.dot_general(gap, users, (((0,), (0,)), ((), ())), precision=PREC)
    return 2.0 * product + 2.0 * ridge_weight * items


def pair_kernel(users_ref, items_ref, tile_ref, gap_ref, grad_ref):
    users, items = users_ref[...], items_ref[...]
    tile = tile_ref[...]
    users_parts = halves(users)
    predicted = product(users_parts, halves(items), ((1,), (1,)))
    prefer = (tile > 0).astype(jnp.float32)
    gap = (1.0 + conf_scale * tile.astype(jnp.float32)) * (predicted - prefer)
    gap_ref[...] = gap
    grad_ref[...] = 2.0 * product(halves(gap), users_parts, ((0,), (0,))) + 2.0 * ridge_weight * items


def pair(users, items, counts, stratum):
    rows = items.shape[0]
    whole = pl.BlockSpec(items.shape, lambda i: (0, 0))
    return pl.pallas_call(
        pair_kernel,
        out_shape=[jax.ShapeDtypeStruct((users.shape[0], rows), jnp.float32), jax.ShapeDtypeStruct(items.shape, jnp.float32)],
        grid=(1,),
        in_specs=[whole, whole, pl.BlockSpec((users.shape[0], rows), lambda i: (0, stratum))],
        out_specs=[whole, whole],
        compiler_params=pltpu.CompilerParams(vmem_limit_bytes=8 * 2**20),
        cost_estimate=pl.CostEstimate(flops=12 * rows**3, bytes_accessed=5 * 4 * rows**2, transcendentals=0),
        name="pair",
    )(users, items, counts)


def user_gradient(gap, users, items):
    return 2.0 * jnp.dot(gap, items, precision=PREC) + 2.0 * ridge_weight * users


def adagrad(factors, sums, gradient):
    sums = sums + gradient * gradient
    return factors - step_rate * gradient / jnp.sqrt(sums), sums


def body(users, user_acc, items, item_acc, counts):
    odd = lax.axis_index("blk") % 2 == 1

    def two_strata(users, user_acc, items, item_acc, first, up):
        if first == 0:
            gap = weighted_gap(users, items, counts[:, : items.shape[0]])
            grad_v = item_gradient(gap, users, items)
        else:
            gap, grad_v = pair(users, items, counts, first)
        grad_u = user_gradient(gap, users, items)
        items, item_acc = adagrad(items, item_acc, grad_v)
        users, user_acc = adagrad(users, user_acc, grad_u)

        visitor = sent(items, lambda b, g: (b + 1, g))
        items, item_acc, users = lax.optimization_barrier((items, item_acc, users))
        ahead = sent(jnp.where(odd, item_acc, items), lambda b, g: (b + 2, g + up))
        even_acc = sent(item_acc, lambda b, g: (b + 2, g + up) if b % 2 == 0 else None)
        passed = sent(visitor, lambda b, g: (b + 1, g + up) if b % 2 == 0 else None)
        gap, grad_v = pair(users, visitor, counts, first + 1)
        grad_u = user_gradient(gap, users, visitor)
        grad_v = sent(grad_v, lambda b, g: (b + 1, g + up))
        users, user_acc = adagrad(users, user_acc, grad_u)
        items = jnp.where(odd, passed, ahead)
        item_acc = jnp.where(odd, ahead, even_acc)
        items, item_acc = adagrad(items, item_acc, grad_v)
        return users, user_acc, items, item_acc

    state = two_strata(users, user_acc, items, item_acc, 0, 0)
    return two_strata(*state, 2, 1)


def solution(mesh):
    spec = P(("blk", "group"), None)
    return jax.shard_map(body, mesh=mesh, in_specs=(spec,) * 5, out_specs=(spec,) * 4, check_vma=False)
```

```python
import jax
import jax.numpy as jnp
from jax import lax
from jax.experimental import pallas as pl
from jax.experimental.pallas import tpu as pltpu
from jax.sharding import PartitionSpec as P

conf_scale = 0.5
ridge_weight = 0.01
step_rate = 0.1

PREC = lax.Precision.HIGH


def sent(value, where):
    n_blk, n_group = lax.axis_size("blk"), lax.axis_size("group")
    pairs = []
    for b in range(n_blk):
        for g in range(n_group):
            target = where(b, g)
            if target is not None:
                pairs.append((b * n_group + g, target[0] % n_blk * n_group + target[1] % n_group))
    return lax.ppermute(value, ("blk", "group"), pairs)


def halves(value):
    high = value.astype(jnp.bfloat16)
    return high, (value - high.astype(jnp.float32)).astype(jnp.bfloat16)


def product(left, right, dims):
    def dot(a, b):
        return lax.dot_general(a, b, (dims, ((), ())), preferred_element_type=jnp.float32)

    return dot(left[0], right[1]) + dot(left[1], right[0]) + dot(left[0], right[0])


def weighted_gap(users, items, count_tile):
    predicted = lax.dot_general(users, items, (((1,), (1,)), ((), ())), precision=PREC)
    prefer = (count_tile > 0).astype(jnp.float32)
    confidence = 1.0 + conf_scale * count_tile.astype(jnp.float32)
    return confidence * (predicted - prefer)


def item_gradient(gap, users, items):
    product = lax.dot_general(gap, users, (((0,), (0,)), ((), ())), precision=PREC)
    return 2.0 * product + 2.0 * ridge_weight * items


def pair_products(users, items, tile):
    users_parts = halves(users)
    predicted = product(users_parts, halves(items), ((1,), (1,)))
    prefer = (tile > 0).astype(jnp.float32)
    gap = (1.0 + conf_scale * tile.astype(jnp.float32)) * (predicted - prefer)
    return gap, 2.0 * product(halves(gap), users_parts, ((0,), (0,))) + 2.0 * ridge_weight * items


def visit_kernel(users_ref, items_ref, tile_ref, gap_ref, grad_ref):
    gap_ref[...], grad_ref[...] = pair_products(users_ref[...], items_ref[...], tile_ref[...])


def local_kernel(
    odd_ref, passed_ref, ahead_ref, even_acc_ref, old_grad_ref, users_ref, tile_ref, items_ref, gap_ref, new_items_ref, new_acc_ref
):
    odd = odd_ref[0] == 1
    ahead = ahead_ref[...]
    items, acc = adagrad(
        jnp.where(odd, passed_ref[...], ahead), jnp.where(odd, ahead, even_acc_ref[...]), old_grad_ref[...]
    )
    gap, grad = pair_products(users_ref[...], items, tile_ref[...])
    items_ref[...], gap_ref[...] = items, gap
    new_items_ref[...], new_acc_ref[...] = adagrad(items, acc, grad)


def on_vmem(kernel, name, outputs, *operands):
    here = pl.BlockSpec(memory_space=pltpu.VMEM)
    scalars = pl.BlockSpec(memory_space=pltpu.SMEM)
    shape = operands[-1].shape
    return pl.pallas_call(
        kernel,
        out_shape=[jax.ShapeDtypeStruct(shape, jnp.float32)] * outputs,
        in_specs=[scalars if operand.ndim == 1 else here for operand in operands],
        out_specs=[here] * outputs,
        compiler_params=pltpu.CompilerParams(vmem_limit_bytes=8 * 2**20),
        cost_estimate=pl.CostEstimate(flops=12 * shape[0] ** 3, bytes_accessed=5 * 4 * shape[0] ** 2, transcendentals=0),
        name=name,
    )(*operands)


def user_gradient(gap, users, items):
    return 2.0 * jnp.dot(gap, items, precision=PREC) + 2.0 * ridge_weight * users


def adagrad(factors, sums, gradient):
    sums = sums + gradient * gradient
    return factors - step_rate * gradient / jnp.sqrt(sums), sums


def body(users, user_acc, items, item_acc, counts):
    rows = items.shape[0]
    tiles = [counts[:, s * rows : (s + 1) * rows] for s in range(4)]
    odd = lax.axis_index("blk") % 2 == 1
    odd_flag = odd.astype(jnp.int32).reshape(1)

    def send_off(users, items, item_acc, up):
        visitor = sent(items, lambda b, g: (b + 1, g))
        items, item_acc, users = lax.optimization_barrier((items, item_acc, users))
        ahead = sent(jnp.where(odd, item_acc, items), lambda b, g: (b + 2, g + up))
        even_acc = sent(item_acc, lambda b, g: (b + 2, g + up) if b % 2 == 0 else None)
        passed = sent(visitor, lambda b, g: (b + 1, g + up) if b % 2 == 0 else None)
        return users, visitor, (passed, ahead, even_acc)

    def visit(users, user_acc, visitor, tile, up):
        gap, grad = on_vmem(visit_kernel, "visit", 2, users, visitor, tile)
        grad = sent(grad, lambda b, g: (b + 1, g + up))
        users, user_acc = adagrad(users, user_acc, user_gradient(gap, users, visitor))
        return users, user_acc, grad

    gap = weighted_gap(users, items, tiles[0])
    new_items, new_acc = adagrad(items, item_acc, item_gradient(gap, users, items))
    users, user_acc = adagrad(users, user_acc, user_gradient(gap, users, items))
    users, visitor, state = send_off(users, new_items, new_acc, 0)
    users, user_acc, grad = visit(users, user_acc, visitor, tiles[1], 0)

    items, gap, new_items, new_acc = on_vmem(local_kernel, "local", 4, odd_flag, *state, grad, users, tiles[2])
    users, user_acc = adagrad(users, user_acc, user_gradient(gap, users, items))
    users, visitor, (passed, ahead, even_acc) = send_off(users, new_items, new_acc, 1)
    users, user_acc, grad = visit(users, user_acc, visitor, tiles[3], 1)

    items, item_acc = adagrad(jnp.where(odd, passed, ahead), jnp.where(odd, ahead, even_acc), grad)
    return users, user_acc, items, item_acc


def solution(mesh):
    spec = P(("blk", "group"), None)
    return jax.shard_map(body, mesh=mesh, in_specs=(spec,) * 5, out_specs=(spec,) * 4, check_vma=False)
```

```python
import jax
import jax.numpy as jnp
from jax import lax
from jax.sharding import PartitionSpec as P

conf_scale = 0.5
ridge_weight = 0.01
step_rate = 0.1

PREC = lax.Precision.HIGH


def sent(value, where):
    n_blk, n_group = lax.axis_size("blk"), lax.axis_size("group")
    pairs = []
    for b in range(n_blk):
        for g in range(n_group):
            target = where(b, g)
            if target is not None:
                pairs.append((b * n_group + g, target[0] % n_blk * n_group + target[1] % n_group))
    return lax.ppermute(value, ("blk", "group"), pairs)


def passes_on(b, g, n_blk):
    return (b % 2 == 1) & ((g % 2 == 1) | (b % n_blk >= n_blk - 2))


def weighted_gap(users, items, count_tile):
    predicted = lax.dot_general(users, items, (((1,), (1,)), ((), ())), precision=PREC)
    prefer = (count_tile > 0).astype(jnp.float32)
    confidence = 1.0 + conf_scale * count_tile.astype(jnp.float32)
    return confidence * (predicted - prefer)


def user_gradient(gap, users, items):
    return 2.0 * jnp.dot(gap, items, precision=PREC) + 2.0 * ridge_weight * users


def item_gradient(gap, users, items):
    product = lax.dot_general(gap, users, (((0,), (0,)), ((), ())), precision=PREC)
    return 2.0 * product + 2.0 * ridge_weight * items


def adagrad(factors, sums, gradient):
    sums = sums + gradient * gradient
    return factors - step_rate * gradient / jnp.sqrt(sums), sums


def body(users, user_acc, items, item_acc, counts):
    rows = items.shape[0]
    tiles = [counts[:, s * rows : (s + 1) * rows] for s in range(4)]
    n_blk, blk, group = lax.axis_size("blk"), lax.axis_index("blk"), lax.axis_index("group")
    passing = passes_on(blk, group, n_blk)

    def two_strata(users, user_acc, items, item_acc, first, up):
        gap = weighted_gap(users, items, tiles[first])
        grad_v = item_gradient(gap, users, items)
        grad_u = user_gradient(gap, users, items)
        items, item_acc = adagrad(items, item_acc, grad_v)
        users, user_acc = adagrad(users, user_acc, grad_u)

        visitor = sent(items, lambda b, g: (b + 1, g))
        items, item_acc, users = lax.optimization_barrier((items, item_acc, users))
        ahead = sent(jnp.where(passing, item_acc, items), lambda b, g: (b + 2, g + up))
        late = sent(item_acc, lambda b, g: None if passes_on(b, g, n_blk) else (b + 2, g + up))
        passed = sent(visitor, lambda b, g: (b + 1, g + up) if passes_on(b - 1, g, n_blk) else None)
        gap = weighted_gap(users, visitor, tiles[first + 1])
        grad_v = item_gradient(gap, users, visitor)
        grad_u = user_gradient(gap, users, visitor)
        grad_v = sent(grad_v, lambda b, g: (b + 1, g + up))
        users, user_acc = adagrad(users, user_acc, grad_u)
        came_by_visit = passes_on((blk - 2) % n_blk, group - up, n_blk)
        items = jnp.where(came_by_visit, passed, ahead)
        item_acc = jnp.where(came_by_visit, ahead, late)
        items, item_acc = adagrad(items, item_acc, grad_v)
        return users, user_acc, items, item_acc

    state = two_strata(users, user_acc, items, item_acc, 0, 0)
    return two_strata(*state, 2, 1)


def solution(mesh):
    spec = P(("blk", "group"), None)
    return jax.shard_map(body, mesh=mesh, in_specs=(spec,) * 5, out_specs=(spec,) * 4, check_vma=False)
```

```python
import jax
import jax.numpy as jnp
from jax import lax
from jax.experimental import pallas as pl
from jax.experimental.pallas import tpu as pltpu
from jax.sharding import PartitionSpec as P

conf_scale = 0.5
ridge_weight = 0.01
step_rate = 0.1

PREC = lax.Precision.HIGH


def sent(value, where):
    n_blk, n_group = lax.axis_size("blk"), lax.axis_size("group")
    pairs = []
    for b in range(n_blk):
        for g in range(n_group):
            target = where(b, g)
            if target is not None:
                pairs.append((b * n_group + g, target[0] % n_blk * n_group + target[1] % n_group))
    return lax.ppermute(value, ("blk", "group"), pairs)


def halves(value):
    high = value.astype(jnp.bfloat16)
    return high, (value - high.astype(jnp.float32)).astype(jnp.bfloat16)


def product(left, right, dims):
    (left_dim,), (right_dim,) = dims
    lefts = jnp.concatenate([left[0], left[0], left[1]], axis=left_dim)
    rights = jnp.concatenate([right[0], right[1], right[0]], axis=right_dim)
    return lax.dot_general(lefts, rights, (dims, ((), ())), preferred_element_type=jnp.float32)


def weighted_gap(users, items, count_tile):
    predicted = lax.dot_general(users, items, (((1,), (1,)), ((), ())), precision=PREC)
    prefer = (count_tile > 0).astype(jnp.float32)
    confidence = 1.0 + conf_scale * count_tile.astype(jnp.float32)
    return confidence * (predicted - prefer)


def item_gradient(gap, users, items):
    product = lax.dot_general(gap, users, (((0,), (0,)), ((), ())), precision=PREC)
    return 2.0 * product + 2.0 * ridge_weight * items


def pair_products(users, items, tile):
    users_parts = halves(users)
    predicted = product(users_parts, halves(items), ((1,), (1,)))
    prefer = (tile > 0).astype(jnp.float32)
    gap = (1.0 + conf_scale * tile.astype(jnp.float32)) * (predicted - prefer)
    return gap, 2.0 * product(halves(gap), users_parts, ((0,), (0,))) + 2.0 * ridge_weight * items


def visit_kernel(users_ref, items_ref, tile_ref, gap_ref, grad_ref):
    gap_ref[...], grad_ref[...] = pair_products(users_ref[...], items_ref[...], tile_ref[...])


def local_kernel(
    odd_ref, passed_ref, ahead_ref, even_acc_ref, old_grad_ref, users_ref, tile_ref, items_ref, gap_ref, new_items_ref, new_acc_ref
):
    odd = odd_ref[0] == 1
    ahead = ahead_ref[...]
    items, acc = adagrad(
        jnp.where(odd, passed_ref[...], ahead), jnp.where(odd, ahead, even_acc_ref[...]), old_grad_ref[...]
    )
    gap, grad = pair_products(users_ref[...], items, tile_ref[...])
    items_ref[...], gap_ref[...] = items, gap
    new_items_ref[...], new_acc_ref[...] = adagrad(items, acc, grad)


def on_vmem(kernel, name, outputs, *operands):
    here = pl.BlockSpec(memory_space=pltpu.VMEM)
    scalars = pl.BlockSpec(memory_space=pltpu.SMEM)
    shape = operands[-1].shape
    return pl.pallas_call(
        kernel,
        out_shape=[jax.ShapeDtypeStruct(shape, jnp.float32)] * outputs,
        in_specs=[scalars if operand.ndim == 1 else here for operand in operands],
        out_specs=[here] * outputs,
        compiler_params=pltpu.CompilerParams(vmem_limit_bytes=8 * 2**20),
        cost_estimate=pl.CostEstimate(flops=12 * shape[0] ** 3, bytes_accessed=5 * 4 * shape[0] ** 2, transcendentals=0),
        name=name,
    )(*operands)


def user_gradient(gap, users, items):
    return 2.0 * jnp.dot(gap, items, precision=PREC) + 2.0 * ridge_weight * users


def adagrad(factors, sums, gradient):
    sums = sums + gradient * gradient
    return factors - step_rate * gradient / jnp.sqrt(sums), sums


def body(users, user_acc, items, item_acc, counts):
    rows = items.shape[0]
    tiles = [counts[:, s * rows : (s + 1) * rows] for s in range(4)]
    odd = lax.axis_index("blk") % 2 == 1
    odd_flag = odd.astype(jnp.int32).reshape(1)

    def send_off(users, items, item_acc, up):
        visitor = sent(items, lambda b, g: (b + 1, g))
        items, item_acc, users = lax.optimization_barrier((items, item_acc, users))
        ahead = sent(jnp.where(odd, item_acc, items), lambda b, g: (b + 2, g + up))
        even_acc = sent(item_acc, lambda b, g: (b + 2, g + up) if b % 2 == 0 else None)
        passed = sent(visitor, lambda b, g: (b + 1, g + up) if b % 2 == 0 else None)
        return users, visitor, (passed, ahead, even_acc)

    def visit(users, user_acc, visitor, tile, up):
        gap, grad = on_vmem(visit_kernel, "visit", 2, users, visitor, tile)
        grad = sent(grad, lambda b, g: (b + 1, g + up))
        users, user_acc = adagrad(users, user_acc, user_gradient(gap, users, visitor))
        return users, user_acc, grad

    gap = weighted_gap(users, items, tiles[0])
    new_items, new_acc = adagrad(items, item_acc, item_gradient(gap, users, items))
    users, user_acc = adagrad(users, user_acc, user_gradient(gap, users, items))
    users, visitor, state = send_off(users, new_items, new_acc, 0)
    users, user_acc, grad = visit(users, user_acc, visitor, tiles[1], 0)

    items, gap, new_items, new_acc = on_vmem(local_kernel, "local", 4, odd_flag, *state, grad, users, tiles[2])
    users, user_acc = adagrad(users, user_acc, user_gradient(gap, users, items))
    users, visitor, (passed, ahead, even_acc) = send_off(users, new_items, new_acc, 1)
    users, user_acc, grad = visit(users, user_acc, visitor, tiles[3], 1)

    items, item_acc = adagrad(jnp.where(odd, passed, ahead), jnp.where(odd, ahead, even_acc), grad)
    return users, user_acc, items, item_acc


def solution(mesh):
    spec = P(("blk", "group"), None)
    return jax.shard_map(body, mesh=mesh, in_specs=(spec,) * 5, out_specs=(spec,) * 4, check_vma=False)
```

```python
import jax
import jax.numpy as jnp
from jax import lax
from jax.experimental import pallas as pl
from jax.experimental.pallas import tpu as pltpu
from jax.sharding import PartitionSpec as P

conf_scale = 0.5
ridge_weight = 0.01
step_rate = 0.1

PREC = lax.Precision.HIGH


def sent(value, where):
    n_blk, n_group = lax.axis_size("blk"), lax.axis_size("group")
    pairs = []
    for b in range(n_blk):
        for g in range(n_group):
            target = where(b, g)
            if target is not None:
                pairs.append((b * n_group + g, target[0] % n_blk * n_group + target[1] % n_group))
    return lax.ppermute(value, ("blk", "group"), pairs)


def weighted_gap(users, items, count_tile):
    predicted = lax.dot_general(users, items, (((1,), (1,)), ((), ())), precision=PREC)
    prefer = (count_tile > 0).astype(jnp.float32)
    confidence = 1.0 + conf_scale * count_tile.astype(jnp.float32)
    return confidence * (predicted - prefer)


def user_gradient(gap, users, items):
    return 2.0 * jnp.dot(gap, items, precision=PREC) + 2.0 * ridge_weight * users


def item_gradient(gap, users, items):
    product = lax.dot_general(gap, users, (((0,), (0,)), ((), ())), precision=PREC)
    return 2.0 * product + 2.0 * ridge_weight * items


def adagrad(factors, sums, gradient):
    sums = sums + gradient * gradient
    return factors - step_rate * gradient / jnp.sqrt(sums), sums


def halves(value):
    high = value.astype(jnp.bfloat16)
    return high, (value - high.astype(jnp.float32)).astype(jnp.bfloat16)


def product(left, right, dims):
    def dot(a, b):
        return lax.dot_general(a, b, (dims, ((), ())), preferred_element_type=jnp.float32)

    return dot(left[0], right[1]) + dot(left[1], right[0]) + dot(left[0], right[0])


def first_kernel(
    users_hbm, items_hbm, counts_hbm, acc_hbm, gap_ref, new_items_ref, new_acc_ref, users_ref, items_ref, tile_ref, acc_ref, done
):
    rows = items_ref.shape[0]
    copies = [
        pltpu.make_async_copy(source, target, done.at[index])
        for index, (source, target) in enumerate(
            [
                (users_hbm, users_ref),
                (items_hbm, items_ref),
                (counts_hbm.at[:, pl.ds(0, rows)], tile_ref),
                (acc_hbm, acc_ref),
            ]
        )
    ]
    for copy in copies:
        copy.start()
    copies[0].wait()
    copies[1].wait()
    items = items_ref[...]
    users_parts = halves(users_ref[...])
    predicted = product(users_parts, halves(items), ((1,), (1,)))
    copies[2].wait()
    tile = tile_ref[...]
    prefer = (tile > 0).astype(jnp.float32)
    gap = (1.0 + conf_scale * tile.astype(jnp.float32)) * (predicted - prefer)
    gap_ref[...] = gap
    grad = 2.0 * product(halves(gap), users_parts, ((0,), (0,))) + 2.0 * ridge_weight * items
    copies[3].wait()
    new_items_ref[...], new_acc_ref[...] = adagrad(items, acc_ref[...], grad)


def first_stratum(*operands):
    users, items, counts, item_acc = operands
    shape, rows = items.shape, items.shape[0]
    here, there = pl.BlockSpec(memory_space=pltpu.VMEM), pl.BlockSpec(memory_space=pltpu.HBM)
    return pl.pallas_call(
        first_kernel,
        out_shape=[jax.ShapeDtypeStruct((users.shape[0], rows), jnp.float32)] + [jax.ShapeDtypeStruct(shape, jnp.float32)] * 2,
        in_specs=[there] * 4,
        out_specs=[here] * 3,
        scratch_shapes=[
            pltpu.VMEM(users.shape, jnp.float32),
            pltpu.VMEM(shape, jnp.float32),
            pltpu.VMEM((users.shape[0], rows), jnp.int32),
            pltpu.VMEM(shape, jnp.float32),
            pltpu.SemaphoreType.DMA((4,)),
        ],
        compiler_params=pltpu.CompilerParams(vmem_limit_bytes=16 * 2**20),
        cost_estimate=pl.CostEstimate(flops=12 * rows**3, bytes_accessed=7 * 4 * rows**2, transcendentals=0),
        name="first_stratum",
    )(*[pltpu.with_memory_space_constraint(operand, pltpu.HBM) for operand in operands])


def body(users, user_acc, items, item_acc, counts):
    rows = items.shape[0]
    tiles = [counts[:, s * rows : (s + 1) * rows] for s in range(4)]
    odd = lax.axis_index("blk") % 2 == 1

    def two_strata(users, user_acc, items, item_acc, first, up):
        if first == 0:
            gap, new_items, item_acc = first_stratum(users, items, counts, item_acc)
        else:
            gap = weighted_gap(users, items, tiles[first])
            new_items, item_acc = adagrad(items, item_acc, item_gradient(gap, users, items))
        grad_u = user_gradient(gap, users, items)
        items = new_items
        users, user_acc = adagrad(users, user_acc, grad_u)

        visitor = sent(items, lambda b, g: (b + 1, g))
        items, item_acc, users = lax.optimization_barrier((items, item_acc, users))
        ahead = sent(jnp.where(odd, item_acc, items), lambda b, g: (b + 2, g + up))
        even_acc = sent(item_acc, lambda b, g: (b + 2, g + up) if b % 2 == 0 else None)
        passed = sent(visitor, lambda b, g: (b + 1, g + up) if b % 2 == 0 else None)
        gap = weighted_gap(users, visitor, tiles[first + 1])
        grad_v = item_gradient(gap, users, visitor)
        grad_u = user_gradient(gap, users, visitor)
        grad_v = sent(grad_v, lambda b, g: (b + 1, g + up))
        users, user_acc = adagrad(users, user_acc, grad_u)
        items = jnp.where(odd, passed, ahead)
        item_acc = jnp.where(odd, ahead, even_acc)
        items, item_acc = adagrad(items, item_acc, grad_v)
        return users, user_acc, items, item_acc

    state = two_strata(users, user_acc, items, item_acc, 0, 0)
    return two_strata(*state, 2, 1)


def solution(mesh):
    spec = P(("blk", "group"), None)
    return jax.shard_map(body, mesh=mesh, in_specs=(spec,) * 5, out_specs=(spec,) * 4, check_vma=False)
```

```python
import jax
import jax.numpy as jnp
from jax import lax
from jax.sharding import PartitionSpec as P

conf_scale = 0.5
ridge_weight = 0.01
step_rate = 0.1

PREC = lax.Precision.HIGH


def sent(value, where):
    n_blk, n_group = lax.axis_size("blk"), lax.axis_size("group")
    pairs = []
    for b in range(n_blk):
        for g in range(n_group):
            target = where(b, g)
            if target is not None:
                pairs.append((b * n_group + g, target[0] % n_blk * n_group + target[1] % n_group))
    return lax.ppermute(value, ("blk", "group"), pairs)


def passes_on(b, g, n_blk, up):
    return (b % 2 == 1) & ((up == 0) | (g % 2 == 1) | (b % n_blk >= n_blk - 2))


def weighted_gap(users, items, count_tile):
    predicted = lax.dot_general(users, items, (((1,), (1,)), ((), ())), precision=PREC)
    prefer = (count_tile > 0).astype(jnp.float32)
    confidence = 1.0 + conf_scale * count_tile.astype(jnp.float32)
    return confidence * (predicted - prefer)


def user_gradient(gap, users, items):
    return 2.0 * jnp.dot(gap, items, precision=PREC) + 2.0 * ridge_weight * users


def item_gradient(gap, users, items):
    product = lax.dot_general(gap, users, (((0,), (0,)), ((), ())), precision=PREC)
    return 2.0 * product + 2.0 * ridge_weight * items


def adagrad(factors, sums, gradient):
    sums = sums + gradient * gradient
    return factors - step_rate * gradient / jnp.sqrt(sums), sums


def body(users, user_acc, items, item_acc, counts):
    rows = items.shape[0]
    tiles = [counts[:, s * rows : (s + 1) * rows] for s in range(4)]
    n_blk, blk, group = lax.axis_size("blk"), lax.axis_index("blk"), lax.axis_index("group")

    def two_strata(users, user_acc, items, item_acc, first, up):
        gap = weighted_gap(users, items, tiles[first])
        grad_v = item_gradient(gap, users, items)
        grad_u = user_gradient(gap, users, items)
        items, item_acc = adagrad(items, item_acc, grad_v)
        users, user_acc = adagrad(users, user_acc, grad_u)

        visitor = sent(items, lambda b, g: (b + 1, g))
        items, item_acc, users = lax.optimization_barrier((items, item_acc, users))
        passing = passes_on(blk, group, n_blk, up)
        ahead = sent(jnp.where(passing, item_acc, items), lambda b, g: (b + 2, g + up))
        late = sent(item_acc, lambda b, g: None if passes_on(b, g, n_blk, up) else (b + 2, g + up))
        passed = sent(visitor, lambda b, g: (b + 1, g + up) if passes_on(b - 1, g, n_blk, up) else None)
        gap = weighted_gap(users, visitor, tiles[first + 1])
        grad_v = item_gradient(gap, users, visitor)
        grad_u = user_gradient(gap, users, visitor)
        grad_v = sent(grad_v, lambda b, g: (b + 1, g + up))
        users, user_acc = adagrad(users, user_acc, grad_u)
        came_by_visit = passes_on((blk - 2) % n_blk, group - up, n_blk, up)
        items = jnp.where(came_by_visit, passed, ahead)
        item_acc = jnp.where(came_by_visit, ahead, late)
        items, item_acc = adagrad(items, item_acc, grad_v)
        return users, user_acc, items, item_acc

    state = two_strata(users, user_acc, items, item_acc, 0, 0)
    return two_strata(*state, 2, 1)


def solution(mesh):
    spec = P(("blk", "group"), None)
    return jax.shard_map(body, mesh=mesh, in_specs=(spec,) * 5, out_specs=(spec,) * 4, check_vma=False)
```

```python
import jax
import jax.numpy as jnp
from jax import lax
from jax.experimental import pallas as pl
from jax.experimental.pallas import tpu as pltpu
from jax.sharding import PartitionSpec as P

conf_scale = 0.5
ridge_weight = 0.01
step_rate = 0.1

PREC = lax.Precision.HIGH


def sent(value, where):
    n_blk, n_group = lax.axis_size("blk"), lax.axis_size("group")
    pairs = []
    for b in range(n_blk):
        for g in range(n_group):
            target = where(b, g)
            if target is not None:
                pairs.append((b * n_group + g, target[0] % n_blk * n_group + target[1] % n_group))
    return lax.ppermute(value, ("blk", "group"), pairs)


def halves(value):
    high = value.astype(jnp.bfloat16)
    return high, (value - high.astype(jnp.float32)).astype(jnp.bfloat16)


def product(left, right, dims):
    (left_dim,), (right_dim,) = dims
    lefts = jnp.concatenate([left[0], left[0], left[1]], axis=left_dim)
    rights = jnp.concatenate([right[0], right[1], right[0]], axis=right_dim)
    return lax.dot_general(lefts, rights, (dims, ((), ())), preferred_element_type=jnp.float32)


def weighted_gap(users, items, count_tile):
    predicted = lax.dot_general(users, items, (((1,), (1,)), ((), ())), precision=PREC)
    prefer = (count_tile > 0).astype(jnp.float32)
    confidence = 1.0 + conf_scale * count_tile.astype(jnp.float32)
    return confidence * (predicted - prefer)


def item_gradient(gap, users, items):
    product = lax.dot_general(gap, users, (((0,), (0,)), ((), ())), precision=PREC)
    return 2.0 * product + 2.0 * ridge_weight * items


def pair_products(users, items, tile):
    users_parts = halves(users)
    predicted = product(users_parts, halves(items), ((1,), (1,)))
    prefer = (tile > 0).astype(jnp.float32)
    gap = (1.0 + conf_scale * tile.astype(jnp.float32)) * (predicted - prefer)
    return gap, 2.0 * product(halves(gap), users_parts, ((0,), (0,))) + 2.0 * ridge_weight * items


def visit_kernel(users_ref, items_ref, tile_ref, gap_ref, grad_ref):
    gap_ref[...], grad_ref[...] = pair_products(users_ref[...], items_ref[...], tile_ref[...])


def local_kernel(
    odd_ref, passed_ref, ahead_ref, even_acc_ref, old_grad_ref, users_ref, tile_ref, items_ref, gap_ref, new_items_ref, new_acc_ref
):
    odd = odd_ref[0] == 1
    ahead = ahead_ref[...]
    items, acc = adagrad(
        jnp.where(odd, passed_ref[...], ahead), jnp.where(odd, ahead, even_acc_ref[...]), old_grad_ref[...]
    )
    gap, grad = pair_products(users_ref[...], items, tile_ref[...])
    items_ref[...], gap_ref[...] = items, gap
    new_items_ref[...], new_acc_ref[...] = adagrad(items, acc, grad)


def last_kernel(odd_ref, passed_ref, ahead_ref, even_acc_ref, grad_ref, items_hbm, acc_hbm, items_ref, acc_ref, done):
    odd = odd_ref[0] == 1
    parts = done.shape[0]
    size = grad_ref.shape[0] // parts
    copies = []
    for part in range(parts):
        at = pl.ds(part * size, size)
        ahead = ahead_ref[at, :]
        items_ref[at, :], acc_ref[at, :] = adagrad(
            jnp.where(odd, passed_ref[at, :], ahead), jnp.where(odd, ahead, even_acc_ref[at, :]), grad_ref[at, :]
        )
        for index, (source, target) in enumerate([(items_ref, items_hbm), (acc_ref, acc_hbm)]):
            copy = pltpu.make_async_copy(source.at[at, :], target.at[at, :], done.at[part, index])
            copy.start()
            copies.append(copy)
    for copy in copies:
        copy.wait()


def last_update(odd_flag, passed, ahead, even_acc, grad):
    here, there = pl.BlockSpec(memory_space=pltpu.VMEM), pl.BlockSpec(memory_space=pltpu.HBM)
    shape = jax.ShapeDtypeStruct(grad.shape, jnp.float32)
    return pl.pallas_call(
        last_kernel,
        out_shape=[shape] * 2,
        in_specs=[pl.BlockSpec(memory_space=pltpu.SMEM)] + [here] * 4,
        out_specs=[there] * 2,
        scratch_shapes=[pltpu.VMEM(grad.shape, jnp.float32)] * 2 + [pltpu.SemaphoreType.DMA((4, 2))],
        compiler_params=pltpu.CompilerParams(vmem_limit_bytes=8 * 2**20),
        cost_estimate=pl.CostEstimate(flops=8 * grad.size, bytes_accessed=24 * grad.size, transcendentals=grad.size),
        name="last_update",
    )(odd_flag, passed, ahead, even_acc, grad)


def on_vmem(kernel, name, outputs, *operands):
    here = pl.BlockSpec(memory_space=pltpu.VMEM)
    scalars = pl.BlockSpec(memory_space=pltpu.SMEM)
    shape = operands[-1].shape
    return pl.pallas_call(
        kernel,
        out_shape=[jax.ShapeDtypeStruct(shape, jnp.float32)] * outputs,
        in_specs=[scalars if operand.ndim == 1 else here for operand in operands],
        out_specs=[here] * outputs,
        compiler_params=pltpu.CompilerParams(vmem_limit_bytes=8 * 2**20),
        cost_estimate=pl.CostEstimate(flops=12 * shape[0] ** 3, bytes_accessed=5 * 4 * shape[0] ** 2, transcendentals=0),
        name=name,
    )(*operands)


def user_gradient(gap, users, items):
    return 2.0 * jnp.dot(gap, items, precision=PREC) + 2.0 * ridge_weight * users


def adagrad(factors, sums, gradient):
    sums = sums + gradient * gradient
    return factors - step_rate * gradient * lax.rsqrt(sums), sums


def body(users, user_acc, items, item_acc, counts):
    rows = items.shape[0]
    tiles = [counts[:, s * rows : (s + 1) * rows] for s in range(4)]
    odd = lax.axis_index("blk") % 2 == 1
    odd_flag = odd.astype(jnp.int32).reshape(1)

    def send_off(users, items, item_acc, up):
        visitor = sent(items, lambda b, g: (b + 1, g))
        items, item_acc, users = lax.optimization_barrier((items, item_acc, users))
        ahead = sent(jnp.where(odd, item_acc, items), lambda b, g: (b + 2, g + up))
        even_acc = sent(item_acc, lambda b, g: (b + 2, g + up) if b % 2 == 0 else None)
        passed = sent(visitor, lambda b, g: (b + 1, g + up) if b % 2 == 0 else None)
        return users, visitor, (passed, ahead, even_acc)

    def visit(users, user_acc, visitor, tile, up):
        gap, grad = on_vmem(visit_kernel, "visit", 2, users, visitor, tile)
        grad = sent(grad, lambda b, g: (b + 1, g + up))
        users, user_acc = adagrad(users, user_acc, user_gradient(gap, users, visitor))
        return users, user_acc, grad

    gap = weighted_gap(users, items, tiles[0])
    new_items, new_acc = adagrad(items, item_acc, item_gradient(gap, users, items))
    users, user_acc = adagrad(users, user_acc, user_gradient(gap, users, items))
    users, visitor, state = send_off(users, new_items, new_acc, 0)
    users, user_acc, grad = visit(users, user_acc, visitor, tiles[1], 0)

    items, gap, new_items, new_acc = on_vmem(local_kernel, "local", 4, odd_flag, *state, grad, users, tiles[2])
    users, user_acc = adagrad(users, user_acc, user_gradient(gap, users, items))
    users, visitor, (passed, ahead, even_acc) = send_off(users, new_items, new_acc, 1)
    users, user_acc, grad = visit(users, user_acc, visitor, tiles[3], 1)

    items, item_acc = last_update(odd_flag, passed, ahead, even_acc, grad)
    return users, user_acc, items, item_acc


def solution(mesh):
    spec = P(("blk", "group"), None)
    return jax.shard_map(body, mesh=mesh, in_specs=(spec,) * 5, out_specs=(spec,) * 4, check_vma=False)
```

```python
import jax
import jax.numpy as jnp
from jax import lax
from jax.experimental import pallas as pl
from jax.experimental.pallas import tpu as pltpu
from jax.sharding import PartitionSpec as P

conf_scale = 0.5
ridge_weight = 0.01
step_rate = 0.1

PREC = lax.Precision.HIGH


def sent(value, where):
    n_blk, n_group = lax.axis_size("blk"), lax.axis_size("group")
    pairs = []
    for b in range(n_blk):
        for g in range(n_group):
            target = where(b, g)
            if target is not None:
                pairs.append((b * n_group + g, target[0] % n_blk * n_group + target[1] % n_group))
    return lax.ppermute(value, ("blk", "group"), pairs)


def passes_on(b, g, n_blk, up):
    return (b % 2 == 1) & ((up == 0) | (g % 2 == 1) | (b % n_blk >= n_blk - 2))


def halves(value):
    high = value.astype(jnp.bfloat16)
    return high, (value - high.astype(jnp.float32)).astype(jnp.bfloat16)


def product(left, right, dims):
    (left_dim,), (right_dim,) = dims
    lefts = jnp.concatenate([left[0], left[0], left[1]], axis=left_dim)
    rights = jnp.concatenate([right[0], right[1], right[0]], axis=right_dim)
    return lax.dot_general(lefts, rights, (dims, ((), ())), preferred_element_type=jnp.float32)


def weighted_gap(users, items, count_tile):
    predicted = lax.dot_general(users, items, (((1,), (1,)), ((), ())), precision=PREC)
    prefer = (count_tile > 0).astype(jnp.float32)
    confidence = 1.0 + conf_scale * count_tile.astype(jnp.float32)
    return confidence * (predicted - prefer)


def item_gradient(gap, users, items):
    product = lax.dot_general(gap, users, (((0,), (0,)), ((), ())), precision=PREC)
    return 2.0 * product + 2.0 * ridge_weight * items


def pair_products(users, items, tile):
    users_parts = halves(users)
    predicted = product(users_parts, halves(items), ((1,), (1,)))
    prefer = (tile > 0).astype(jnp.float32)
    gap = (1.0 + conf_scale * tile.astype(jnp.float32)) * (predicted - prefer)
    return gap, 2.0 * product(halves(gap), users_parts, ((0,), (0,))) + 2.0 * ridge_weight * items


def visit_kernel(users_ref, items_ref, tile_ref, gap_ref, grad_ref):
    gap_ref[...], grad_ref[...] = pair_products(users_ref[...], items_ref[...], tile_ref[...])


def local_kernel(
    by_visit_ref, passed_ref, ahead_ref, late_ref, old_grad_ref, users_ref, tile_ref, items_ref, gap_ref, new_items_ref, new_acc_ref
):
    by_visit = by_visit_ref[0] == 1
    ahead = ahead_ref[...]
    items, acc = adagrad(
        jnp.where(by_visit, passed_ref[...], ahead), jnp.where(by_visit, ahead, late_ref[...]), old_grad_ref[...]
    )
    gap, grad = pair_products(users_ref[...], items, tile_ref[...])
    items_ref[...], gap_ref[...] = items, gap
    new_items_ref[...], new_acc_ref[...] = adagrad(items, acc, grad)


def last_kernel(by_visit_ref, passed_ref, ahead_ref, late_ref, grad_ref, items_hbm, acc_hbm, items_ref, acc_ref, done):
    by_visit = by_visit_ref[0] == 1
    parts = done.shape[0]
    size = grad_ref.shape[0] // parts
    copies = []
    for part in range(parts):
        at = pl.ds(part * size, size)
        ahead = ahead_ref[at, :]
        items_ref[at, :], acc_ref[at, :] = adagrad(
            jnp.where(by_visit, passed_ref[at, :], ahead), jnp.where(by_visit, ahead, late_ref[at, :]), grad_ref[at, :]
        )
        for index, (source, target) in enumerate([(items_ref, items_hbm), (acc_ref, acc_hbm)]):
            copy = pltpu.make_async_copy(source.at[at, :], target.at[at, :], done.at[part, index])
            copy.start()
            copies.append(copy)
    for copy in copies:
        copy.wait()


def last_update(by_visit, passed, ahead, late, grad):
    here, there = pl.BlockSpec(memory_space=pltpu.VMEM), pl.BlockSpec(memory_space=pltpu.HBM)
    shape = jax.ShapeDtypeStruct(grad.shape, jnp.float32)
    return pl.pallas_call(
        last_kernel,
        out_shape=[shape] * 2,
        in_specs=[pl.BlockSpec(memory_space=pltpu.SMEM)] + [here] * 4,
        out_specs=[there] * 2,
        scratch_shapes=[pltpu.VMEM(grad.shape, jnp.float32)] * 2 + [pltpu.SemaphoreType.DMA((4, 2))],
        compiler_params=pltpu.CompilerParams(vmem_limit_bytes=8 * 2**20),
        cost_estimate=pl.CostEstimate(flops=8 * grad.size, bytes_accessed=24 * grad.size, transcendentals=grad.size),
        name="last_update",
    )(by_visit, passed, ahead, late, grad)


def on_vmem(kernel, name, outputs, *operands):
    here = pl.BlockSpec(memory_space=pltpu.VMEM)
    scalars = pl.BlockSpec(memory_space=pltpu.SMEM)
    shape = operands[-1].shape
    return pl.pallas_call(
        kernel,
        out_shape=[jax.ShapeDtypeStruct(shape, jnp.float32)] * outputs,
        in_specs=[scalars if operand.ndim == 1 else here for operand in operands],
        out_specs=[here] * outputs,
        compiler_params=pltpu.CompilerParams(vmem_limit_bytes=8 * 2**20),
        cost_estimate=pl.CostEstimate(flops=12 * shape[0] ** 3, bytes_accessed=5 * 4 * shape[0] ** 2, transcendentals=0),
        name=name,
    )(*operands)


def user_gradient(gap, users, items):
    return 2.0 * jnp.dot(gap, items, precision=PREC) + 2.0 * ridge_weight * users


def adagrad(factors, sums, gradient):
    sums = sums + gradient * gradient
    return factors - step_rate * gradient * lax.rsqrt(sums), sums


def body(users, user_acc, items, item_acc, counts):
    rows = items.shape[0]
    tiles = [counts[:, s * rows : (s + 1) * rows] for s in range(4)]
    n_blk, blk, group = lax.axis_size("blk"), lax.axis_index("blk"), lax.axis_index("group")

    def send_off(users, items, item_acc, up):
        visitor = sent(items, lambda b, g: (b + 1, g))
        items, item_acc, users = lax.optimization_barrier((items, item_acc, users))
        passing = passes_on(blk, group, n_blk, up)
        ahead = sent(jnp.where(passing, item_acc, items), lambda b, g: (b + 2, g + up))
        late = sent(item_acc, lambda b, g: None if passes_on(b, g, n_blk, up) else (b + 2, g + up))
        passed = sent(visitor, lambda b, g: (b + 1, g + up) if passes_on(b - 1, g, n_blk, up) else None)
        came_by_visit = passes_on((blk - 2) % n_blk, group - up, n_blk, up)
        return users, visitor, (came_by_visit.astype(jnp.int32).reshape(1), passed, ahead, late)

    def visit(users, user_acc, visitor, tile, up):
        gap, grad = on_vmem(visit_kernel, "visit", 2, users, visitor, tile)
        grad = sent(grad, lambda b, g: (b + 1, g + up))
        users, user_acc = adagrad(users, user_acc, user_gradient(gap, users, visitor))
        return users, user_acc, grad

    gap = weighted_gap(users, items, tiles[0])
    new_items, new_acc = adagrad(items, item_acc, item_gradient(gap, users, items))
    users, user_acc = adagrad(users, user_acc, user_gradient(gap, users, items))
    users, visitor, state = send_off(users, new_items, new_acc, 0)
    users, user_acc, grad = visit(users, user_acc, visitor, tiles[1], 0)

    items, gap, new_items, new_acc = on_vmem(local_kernel, "local", 4, *state, grad, users, tiles[2])
    users, user_acc = adagrad(users, user_acc, user_gradient(gap, users, items))
    users, visitor, state = send_off(users, new_items, new_acc, 1)
    users, user_acc, grad = visit(users, user_acc, visitor, tiles[3], 1)

    items, item_acc = last_update(*state, grad)
    return users, user_acc, items, item_acc


def solution(mesh):
    spec = P(("blk", "group"), None)
    return jax.shard_map(body, mesh=mesh, in_specs=(spec,) * 5, out_specs=(spec,) * 4, check_vma=False)
```

```python
import jax
import jax.numpy as jnp
from jax import lax
from jax.experimental import pallas as pl
from jax.experimental.pallas import tpu as pltpu
from jax.sharding import PartitionSpec as P

conf_scale = 0.5
ridge_weight = 0.01
step_rate = 0.1

PREC = lax.Precision.HIGH


def sent(value, where):
    n_blk, n_group = lax.axis_size("blk"), lax.axis_size("group")
    pairs = []
    for b in range(n_blk):
        for g in range(n_group):
            target = where(b, g)
            if target is not None:
                pairs.append((b * n_group + g, target[0] % n_blk * n_group + target[1] % n_group))
    return lax.ppermute(value, ("blk", "group"), pairs)


def passes_on(b, g, up):
    return (b % 2 == 1) & ((up == 0) | (g % 2 == 1))


def halves(value):
    high = value.astype(jnp.bfloat16)
    return high, (value - high.astype(jnp.float32)).astype(jnp.bfloat16)


def product(left, right, dims):
    (left_dim,), (right_dim,) = dims
    lefts = jnp.concatenate([left[0], left[0], left[1]], axis=left_dim)
    rights = jnp.concatenate([right[0], right[1], right[0]], axis=right_dim)
    return lax.dot_general(lefts, rights, (dims, ((), ())), preferred_element_type=jnp.float32)


def weighted_gap(users, items, count_tile):
    predicted = lax.dot_general(users, items, (((1,), (1,)), ((), ())), precision=PREC)
    prefer = (count_tile > 0).astype(jnp.float32)
    confidence = 1.0 + conf_scale * count_tile.astype(jnp.float32)
    return confidence * (predicted - prefer)


def item_gradient(gap, users, items):
    product = lax.dot_general(gap, users, (((0,), (0,)), ((), ())), precision=PREC)
    return 2.0 * product + 2.0 * ridge_weight * items


def pair_products(users, items, tile):
    users_parts = halves(users)
    predicted = product(users_parts, halves(items), ((1,), (1,)))
    prefer = (tile > 0).astype(jnp.float32)
    gap = (1.0 + conf_scale * tile.astype(jnp.float32)) * (predicted - prefer)
    return gap, 2.0 * product(halves(gap), users_parts, ((0,), (0,))) + 2.0 * ridge_weight * items


def visit_kernel(users_ref, items_ref, tile_ref, gap_ref, grad_ref):
    gap_ref[...], grad_ref[...] = pair_products(users_ref[...], items_ref[...], tile_ref[...])


def local_kernel(
    by_visit_ref, passed_ref, ahead_ref, late_ref, old_grad_ref, users_ref, tile_ref, items_ref, gap_ref, new_items_ref, new_acc_ref
):
    by_visit = by_visit_ref[0] == 1
    ahead = ahead_ref[...]
    items, acc = adagrad(
        jnp.where(by_visit, passed_ref[...], ahead), jnp.where(by_visit, ahead, late_ref[...]), old_grad_ref[...]
    )
    gap, grad = pair_products(users_ref[...], items, tile_ref[...])
    items_ref[...], gap_ref[...] = items, gap
    new_items_ref[...], new_acc_ref[...] = adagrad(items, acc, grad)


def last_kernel(by_visit_ref, passed_ref, ahead_ref, late_ref, grad_ref, items_hbm, acc_hbm, items_ref, acc_ref, done):
    by_visit = by_visit_ref[0] == 1
    parts = done.shape[0]
    size = grad_ref.shape[0] // parts
    copies = []
    for part in range(parts):
        at = pl.ds(part * size, size)
        ahead = ahead_ref[at, :]
        items_ref[at, :], acc_ref[at, :] = adagrad(
            jnp.where(by_visit, passed_ref[at, :], ahead), jnp.where(by_visit, ahead, late_ref[at, :]), grad_ref[at, :]
        )
        for index, (source, target) in enumerate([(items_ref, items_hbm), (acc_ref, acc_hbm)]):
            copy = pltpu.make_async_copy(source.at[at, :], target.at[at, :], done.at[part, index])
            copy.start()
            copies.append(copy)
    for copy in copies:
        copy.wait()


def last_update(by_visit, passed, ahead, late, grad):
    here, there = pl.BlockSpec(memory_space=pltpu.VMEM), pl.BlockSpec(memory_space=pltpu.HBM)
    shape = jax.ShapeDtypeStruct(grad.shape, jnp.float32)
    return pl.pallas_call(
        last_kernel,
        out_shape=[shape] * 2,
        in_specs=[pl.BlockSpec(memory_space=pltpu.SMEM)] + [here] * 4,
        out_specs=[there] * 2,
        scratch_shapes=[pltpu.VMEM(grad.shape, jnp.float32)] * 2 + [pltpu.SemaphoreType.DMA((4, 2))],
        compiler_params=pltpu.CompilerParams(vmem_limit_bytes=8 * 2**20),
        cost_estimate=pl.CostEstimate(flops=8 * grad.size, bytes_accessed=24 * grad.size, transcendentals=grad.size),
        name="last_update",
    )(by_visit, passed, ahead, late, grad)


def on_vmem(kernel, name, outputs, *operands):
    here = pl.BlockSpec(memory_space=pltpu.VMEM)
    scalars = pl.BlockSpec(memory_space=pltpu.SMEM)
    shape = operands[-1].shape
    return pl.pallas_call(
        kernel,
        out_shape=[jax.ShapeDtypeStruct(shape, jnp.float32)] * outputs,
        in_specs=[scalars if operand.ndim == 1 else here for operand in operands],
        out_specs=[here] * outputs,
        compiler_params=pltpu.CompilerParams(vmem_limit_bytes=8 * 2**20),
        cost_estimate=pl.CostEstimate(flops=12 * shape[0] ** 3, bytes_accessed=5 * 4 * shape[0] ** 2, transcendentals=0),
        name=name,
    )(*operands)


def user_gradient(gap, users, items):
    return 2.0 * jnp.dot(gap, items, precision=PREC) + 2.0 * ridge_weight * users


def adagrad(factors, sums, gradient):
    sums = sums + gradient * gradient
    return factors - step_rate * gradient * lax.rsqrt(sums), sums


def body(users, user_acc, items, item_acc, counts):
    rows = items.shape[0]
    tiles = [counts[:, s * rows : (s + 1) * rows] for s in range(4)]
    blk, group = lax.axis_index("blk"), lax.axis_index("group")

    def send_off(users, items, item_acc, up):
        visitor = sent(items, lambda b, g: (b + 1, g))
        items, item_acc, users = lax.optimization_barrier((items, item_acc, users))
        passing = passes_on(blk, group, up)
        ahead = sent(jnp.where(passing, item_acc, items), lambda b, g: (b + 2, g + up))
        late = sent(item_acc, lambda b, g: None if passes_on(b, g, up) else (b + 2, g + up))
        passed = sent(visitor, lambda b, g: (b + 1, g + up) if passes_on(b - 1, g, up) else None)
        came_by_visit = passes_on(blk, group - up, up)
        return users, visitor, (came_by_visit.astype(jnp.int32).reshape(1), passed, ahead, late)

    def visit(users, user_acc, visitor, tile, up):
        gap, grad = on_vmem(visit_kernel, "visit", 2, users, visitor, tile)
        grad = sent(grad, lambda b, g: (b + 1, g + up))
        users, user_acc = adagrad(users, user_acc, user_gradient(gap, users, visitor))
        return users, user_acc, grad

    gap = weighted_gap(users, items, tiles[0])
    new_items, new_acc = adagrad(items, item_acc, item_gradient(gap, users, items))
    users, user_acc = adagrad(users, user_acc, user_gradient(gap, users, items))
    users, visitor, state = send_off(users, new_items, new_acc, 0)
    users, user_acc, grad = visit(users, user_acc, visitor, tiles[1], 0)

    items, gap, new_items, new_acc = on_vmem(local_kernel, "local", 4, *state, grad, users, tiles[2])
    users, user_acc = adagrad(users, user_acc, user_gradient(gap, users, items))
    users, visitor, state = send_off(users, new_items, new_acc, 1)
    users, user_acc, grad = visit(users, user_acc, visitor, tiles[3], 1)

    items, item_acc = last_update(*state, grad)
    return users, user_acc, items, item_acc


def solution(mesh):
    spec = P(("blk", "group"), None)
    return jax.shard_map(body, mesh=mesh, in_specs=(spec,) * 5, out_specs=(spec,) * 4, check_vma=False)
```

```python
import jax
import jax.numpy as jnp
from jax import lax
from jax.experimental import pallas as pl
from jax.experimental.pallas import tpu as pltpu
from jax.sharding import PartitionSpec as P

conf_scale = 0.5
ridge_weight = 0.01
step_rate = 0.1

PREC = lax.Precision.HIGH


def sent(value, where):
    n_blk, n_group = lax.axis_size("blk"), lax.axis_size("group")
    pairs = []
    for b in range(n_blk):
        for g in range(n_group):
            target = where(b, g)
            if target is not None:
                pairs.append((b * n_group + g, target[0] % n_blk * n_group + target[1] % n_group))
    return lax.ppermute(value, ("blk", "group"), pairs)


def passes_on(b, g, n_blk, up):
    return (b % 2 == 1) & ((up == 0) | ((g % 2 == 1) ^ (b % n_blk >= n_blk - 2)))


def halves(value):
    high = value.astype(jnp.bfloat16)
    return high, (value - high.astype(jnp.float32)).astype(jnp.bfloat16)


def product(left, right, dims):
    (left_dim,), (right_dim,) = dims
    lefts = jnp.concatenate([left[0], left[0], left[1]], axis=left_dim)
    rights = jnp.concatenate([right[0], right[1], right[0]], axis=right_dim)
    return lax.dot_general(lefts, rights, (dims, ((), ())), preferred_element_type=jnp.float32)


def weighted_gap(users, items, count_tile):
    predicted = lax.dot_general(users, items, (((1,), (1,)), ((), ())), precision=PREC)
    prefer = (count_tile > 0).astype(jnp.float32)
    confidence = 1.0 + conf_scale * count_tile.astype(jnp.float32)
    return confidence * (predicted - prefer)


def item_gradient(gap, users, items):
    product = lax.dot_general(gap, users, (((0,), (0,)), ((), ())), precision=PREC)
    return 2.0 * product + 2.0 * ridge_weight * items


def pair_products(users, items, tile):
    users_parts = halves(users)
    predicted = product(users_parts, halves(items), ((1,), (1,)))
    prefer = (tile > 0).astype(jnp.float32)
    gap = (1.0 + conf_scale * tile.astype(jnp.float32)) * (predicted - prefer)
    return gap, 2.0 * product(halves(gap), users_parts, ((0,), (0,))) + 2.0 * ridge_weight * items


def visit_kernel(users_ref, items_ref, tile_ref, gap_ref, grad_ref):
    gap_ref[...], grad_ref[...] = pair_products(users_ref[...], items_ref[...], tile_ref[...])


def local_kernel(
    by_visit_ref, passed_ref, ahead_ref, late_ref, old_grad_ref, users_ref, tile_ref, items_ref, gap_ref, new_items_ref, new_acc_ref
):
    by_visit = by_visit_ref[0] == 1
    ahead = ahead_ref[...]
    items, acc = adagrad(
        jnp.where(by_visit, passed_ref[...], ahead), jnp.where(by_visit, ahead, late_ref[...]), old_grad_ref[...]
    )
    gap, grad = pair_products(users_ref[...], items, tile_ref[...])
    items_ref[...], gap_ref[...] = items, gap
    new_items_ref[...], new_acc_ref[...] = adagrad(items, acc, grad)


def last_kernel(by_visit_ref, passed_ref, ahead_ref, late_ref, grad_ref, items_hbm, acc_hbm, items_ref, acc_ref, done):
    by_visit = by_visit_ref[0] == 1
    parts = done.shape[0]
    size = grad_ref.shape[0] // parts
    copies = []
    for part in range(parts):
        at = pl.ds(part * size, size)
        ahead = ahead_ref[at, :]
        items_ref[at, :], acc_ref[at, :] = adagrad(
            jnp.where(by_visit, passed_ref[at, :], ahead), jnp.where(by_visit, ahead, late_ref[at, :]), grad_ref[at, :]
        )
        for index, (source, target) in enumerate([(items_ref, items_hbm), (acc_ref, acc_hbm)]):
            copy = pltpu.make_async_copy(source.at[at, :], target.at[at, :], done.at[part, index])
            copy.start()
            copies.append(copy)
    for copy in copies:
        copy.wait()


def last_update(by_visit, passed, ahead, late, grad):
    here, there = pl.BlockSpec(memory_space=pltpu.VMEM), pl.BlockSpec(memory_space=pltpu.HBM)
    shape = jax.ShapeDtypeStruct(grad.shape, jnp.float32)
    return pl.pallas_call(
        last_kernel,
        out_shape=[shape] * 2,
        in_specs=[pl.BlockSpec(memory_space=pltpu.SMEM)] + [here] * 4,
        out_specs=[there] * 2,
        scratch_shapes=[pltpu.VMEM(grad.shape, jnp.float32)] * 2 + [pltpu.SemaphoreType.DMA((4, 2))],
        compiler_params=pltpu.CompilerParams(vmem_limit_bytes=8 * 2**20),
        cost_estimate=pl.CostEstimate(flops=8 * grad.size, bytes_accessed=24 * grad.size, transcendentals=grad.size),
        name="last_update",
    )(by_visit, passed, ahead, late, grad)


def on_vmem(kernel, name, outputs, *operands):
    here = pl.BlockSpec(memory_space=pltpu.VMEM)
    scalars = pl.BlockSpec(memory_space=pltpu.SMEM)
    shape = operands[-1].shape
    return pl.pallas_call(
        kernel,
        out_shape=[jax.ShapeDtypeStruct(shape, jnp.float32)] * outputs,
        in_specs=[scalars if operand.ndim == 1 else here for operand in operands],
        out_specs=[here] * outputs,
        compiler_params=pltpu.CompilerParams(vmem_limit_bytes=8 * 2**20),
        cost_estimate=pl.CostEstimate(flops=12 * shape[0] ** 3, bytes_accessed=5 * 4 * shape[0] ** 2, transcendentals=0),
        name=name,
    )(*operands)


def user_gradient(gap, users, items):
    return 2.0 * jnp.dot(gap, items, precision=PREC) + 2.0 * ridge_weight * users


def adagrad(factors, sums, gradient):
    sums = sums + gradient * gradient
    return factors - step_rate * gradient * lax.rsqrt(sums), sums


def body(users, user_acc, items, item_acc, counts):
    rows = items.shape[0]
    tiles = [counts[:, s * rows : (s + 1) * rows] for s in range(4)]
    n_blk, blk, group = lax.axis_size("blk"), lax.axis_index("blk"), lax.axis_index("group")

    def send_off(users, items, item_acc, up):
        visitor = sent(items, lambda b, g: (b + 1, g))
        items, item_acc, users = lax.optimization_barrier((items, item_acc, users))
        passing = passes_on(blk, group, n_blk, up)
        ahead = sent(jnp.where(passing, item_acc, items), lambda b, g: (b + 2, g + up))
        late = sent(item_acc, lambda b, g: None if passes_on(b, g, n_blk, up) else (b + 2, g + up))
        passed = sent(visitor, lambda b, g: (b + 1, g + up) if passes_on(b - 1, g, n_blk, up) else None)
        came_by_visit = passes_on((blk - 2) % n_blk, group - up, n_blk, up)
        return users, visitor, (came_by_visit.astype(jnp.int32).reshape(1), passed, ahead, late)

    def visit(users, user_acc, visitor, tile, up):
        gap, grad = on_vmem(visit_kernel, "visit", 2, users, visitor, tile)
        grad = sent(grad, lambda b, g: (b + 1, g + up))
        users, user_acc = adagrad(users, user_acc, user_gradient(gap, users, visitor))
        return users, user_acc, grad

    gap = weighted_gap(users, items, tiles[0])
    new_items, new_acc = adagrad(items, item_acc, item_gradient(gap, users, items))
    users, user_acc = adagrad(users, user_acc, user_gradient(gap, users, items))
    users, visitor, state = send_off(users, new_items, new_acc, 0)
    users, user_acc, grad = visit(users, user_acc, visitor, tiles[1], 0)

    items, gap, new_items, new_acc = on_vmem(local_kernel, "local", 4, *state, grad, users, tiles[2])
    users, user_acc = adagrad(users, user_acc, user_gradient(gap, users, items))
    users, visitor, state = send_off(users, new_items, new_acc, 1)
    users, user_acc, grad = visit(users, user_acc, visitor, tiles[3], 1)

    items, item_acc = last_update(*state, grad)
    return users, user_acc, items, item_acc


def solution(mesh):
    spec = P(("blk", "group"), None)
    return jax.shard_map(body, mesh=mesh, in_specs=(spec,) * 5, out_specs=(spec,) * 4, check_vma=False)
```
